32 devices in a mesh: member: 2 (over x), space: 8 (over z, y), cuts: 2 (over core).
Axes of the slice: x: 2, y: 2, z: 4, core: 2. Of those that a mesh axis runs over, the one named last changes fastest.
Arguments:
- depth_class: int32 [64, 2048], P('space'), may hold values from 0 to 7
- coef_table: float32 [2, 8], replicated, may hold values from 0.3 to 2
- step_counts: int32 [2], replicated, may hold values from 9 to 12, as said below
- closure_weights: float32 [18, 3, 3], P('member'), parts along dimension 0, may hold values from -1.25 to 1.25
- checkpoints: float32 [4, 3, 64, 2048], P(('member', 'cuts'), None, 'space'), parts along dimension 0, may hold values from -6 to 6
- old_adjoint: float32 [4, 3, 64, 2048], P(('member', 'cuts'), None, 'space'), parts along dimension 0, may hold values from -6 to 6
Outputs:
- new_adjoint: float32 [4, 3, 64, 2048], P(('member', 'cuts'), None, 'space'), parts along dimension 0
- closure_grad: float32 [18, 3, 3], P('member'), parts along dimension 0
The draws below stay inside these ranges and needn't reach their ends.
There are 2 independent parts, one for each index of `member`. The reference program is written for one: setup_inputs(seed, part) draws one part's arguments, and reference() takes and returns one part's arrays. A program takes and returns all parts, laid end to end along the dimension named above; an argument that names none is the same for every part. Nothing has to cross between parts.
Inputs may be any that keep to these rules, and one draw needn't show every extreme that they name: `step_counts`: some slice takes exactly 12 steps.
All inputs are finite; a program needn't handle non-finite values.
Results may differ from the reference program's by a relative error of at most 0.00026.
Values sent between devices are 32-bit elements; how exact they have to be, the bound alone decides.
A program may use at most 128 MiB of HBM per device.

```python
import jax
import jax.numpy as jnp
from jax import lax

COLS = 2048
FINE = 12
CLASSES = 8
SLICES = 2
NX = 64


def draw_step_counts(key, part):
    key = jax.random.fold_in(key, 7)
    first_key, second_key = jax.random.split(key)
    totals = jax.random.randint(first_key, (SLICES,), 3 * FINE // 4, FINE + 1)
    chosen = jax.random.randint(second_key, (), 0, SLICES)
    return jnp.where(jnp.arange(SLICES) == chosen, FINE, totals).astype(jnp.int32)


def touch_ends(array, stream_key, smallest, top_value):
    longest = array.shape.index(max(array.shape))
    spots = []
    for shift in (0, 1):
        where = [jax.random.randint(jax.random.fold_in(stream_key, axis), (), 0, length) for axis, length in enumerate(array.shape)]
        where[longest] = (where[longest] + shift) % array.shape[longest]
        spots.append(tuple(where))
    return array.at[spots[0]].set(smallest).at[spots[1]].set(top_value)


def block_levels(key, dims, cuts, least, largest):
    factor_of, own = 1.0, jax.random.fold_in(key, 6)
    for axis_at, parts in cuts:
        heights = jnp.exp(jax.random.uniform(jax.random.fold_in(own, axis_at), (parts,), jnp.float32, least / len(cuts), largest / len(cuts)))
        factor_of = factor_of * jnp.repeat(heights, dims[axis_at] // parts).reshape([-1 if axis == axis_at else 1 for axis in range(len(dims))])
    return factor_of


def centred(stream_key, dims, scale, bound, pieces=(), dtype=jnp.bfloat16):
    values = scale * jax.random.normal(stream_key, dims, jnp.float32)
    if pieces:
        values = values * block_levels(stream_key, dims, pieces, -0.22, 0.18)
    return jnp.clip(values, -bound, bound).astype(dtype)


def setup_inputs(seed: int = 0, part: int = 0) -> dict:
    keys = jax.random.split(jax.random.key(seed), 7)
    own_keys = jax.random.split(jax.random.fold_in(keys[6], part), 7)
    depth_class = touch_ends(jax.random.randint(keys[0], (NX, COLS), 0, CLASSES), jax.random.fold_in(keys[0], 1), 0, CLASSES - 1).astype(jnp.int32)
    coef_table = jnp.clip(jax.random.uniform(keys[1], (2, CLASSES), jnp.float32, 0.3, 2.0), 0.3, 2.0)
    step_counts = draw_step_counts(jax.random.fold_in(keys[6], 71), part)
    closure_weights = centred(own_keys[3], (9, 3, 3), 0.2, 1.25, (), jnp.float32)
    checkpoints = centred(own_keys[4], (SLICES, 3, NX, COLS), 1.0, 6.0, ((0, 2), (2, 8)), jnp.float32)
    old_adjoint = centred(own_keys[5], (SLICES, 3, NX, COLS), 1.0, 6.0, ((0, 2), (2, 8)), jnp.float32)
    return dict(depth_class=depth_class, coef_table=coef_table, step_counts=step_counts, closure_weights=closure_weights, checkpoints=checkpoints, old_adjoint=old_adjoint)


fine_rate = 0.05
highest = lax.Precision.HIGHEST

def offset_view(widened, offset_row, offset_col, row_count, col_count):
    return widened[:, 1 + offset_row:1 + offset_row + row_count, 1 + offset_col:1 + offset_col + col_count]

def advance(padded, depth_field, friction, weights, step_rate):
    row_count = padded.shape[1] - 2
    col_count = padded.shape[2]
    widened = jnp.pad(padded, ((0, 0), (0, 0), (1, 1)))
    centre = offset_view(widened, 0, 0, row_count, col_count)
    to_east = offset_view(widened, 0, 1, row_count, col_count)
    to_west = offset_view(widened, 0, -1, row_count, col_count)
    to_north = offset_view(widened, 1, 0, row_count, col_count)
    to_south = offset_view(widened, -1, 0, row_count, col_count)
    spread = 0.5 * (to_east[1] - to_west[1] + (to_north[2] - to_south[2]))
    height = centre[0] - step_rate * depth_field * spread
    along_x = centre[1] - step_rate * (0.5 * (to_east[0] - to_west[0]) + friction * centre[1])
    along_y = centre[2] - step_rate * (0.5 * (to_north[0] - to_south[0]) + friction * centre[2])
    closure = jnp.zeros_like(centre)
    for offset_row in (-1, 0, 1):
        for offset_col in (-1, 0, 1):
            stencil_index = 3 * (offset_row + 1) + offset_col + 1
            closure = closure + jnp.einsum('oc,cij->oij', weights[stencil_index], offset_view(widened, offset_row, offset_col, row_count, col_count), precision=highest)
    return jnp.stack([height, along_x, along_y]) + step_rate * closure

def pad_rows(field, rim_width):
    return jnp.pad(field, ((0, 0), (rim_width, rim_width), (0, 0)))

def transpose_step(adjoint, depth_field, friction, weights, step_rate):

    def forward(state_now):
        return advance(pad_rows(state_now, 1), depth_field, friction, weights, step_rate)
    _, pullback = jax.vjp(forward, jnp.zeros_like(adjoint))
    return pullback(adjoint)[0]

def closure_terms(adjoint, padded, step_rate):
    row_count = adjoint.shape[1]
    col_count = adjoint.shape[2]
    widened = jnp.pad(padded, ((0, 0), (0, 0), (1, 1)))
    terms = []
    for offset_row in (-1, 0, 1):
        for offset_col in (-1, 0, 1):
            shifted = offset_view(widened, offset_row, offset_col, row_count, col_count)
            terms.append(jnp.einsum('oij,cij->oc', adjoint, shifted, precision=highest))
    return step_rate * jnp.stack(terms)

def reference(depth_class, coef_table, step_counts, closure_weights, checkpoints, old_adjoint):
    depth_field = coef_table[0][depth_class]
    friction = coef_table[1][depth_class]
    gradient = jnp.zeros((9, 3, 3), jnp.float32)
    differences = []
    coarse_rates = []
    for slice_index in range(SLICES):
        step_total = step_counts[slice_index]
        state_now = checkpoints[slice_index]
        history = []
        for step_index in range(FINE):
            history.append(state_now)
            stepped = advance(pad_rows(state_now, 1), depth_field, friction, closure_weights, fine_rate)
            state_now = jnp.where(step_index < step_total, stepped, state_now)
        adjoint = old_adjoint[slice_index]
        for step_index in reversed(range(FINE)):
            active = step_index < step_total
            gradient = gradient + jnp.where(active, closure_terms(adjoint, pad_rows(history[step_index], 1), fine_rate), 0.0)
            pulled = transpose_step(adjoint, depth_field, friction, closure_weights, fine_rate)
            adjoint = jnp.where(active, pulled, adjoint)
        coarse_rate = step_total.astype(jnp.float32) * fine_rate
        coarse_rates.append(coarse_rate)
        differences.append(adjoint - transpose_step(old_adjoint[slice_index], depth_field, friction, closure_weights, coarse_rate))
    ending = old_adjoint[SLICES - 1]
    starts = [None] * SLICES
    for slice_index in reversed(range(SLICES)):
        beginning = transpose_step(ending, depth_field, friction, closure_weights, coarse_rates[slice_index]) + differences[slice_index]
        starts[slice_index] = beginning
        ending = beginning
    grad_scale = float(NX * COLS * SLICES) ** (-0.5)
    return (jnp.stack(starts), gradient * grad_scale)
```

```python
import functools

import jax
import jax.numpy as jnp
from jax import lax
from jax.experimental import pallas as pl
from jax.experimental.pallas import tpu as pltpu
from jax.sharding import PartitionSpec as P

FINE = 12
fine_rate = 0.05
LANES = 128
HALF = LANES // 2
MESH = pl.DeviceIdType.MESH
BLOCK = 2
GRAD_BLOCK = 2


def kernel(
    geo,
    depth_ref, table_ref, counts_ref, weights_ref, state_ref, adjoint_ref,
    out_ref, grad_ref,
    send_adj, send_state, recv_adj, recv_state, depth_half, depth_east, depth_west, friction,
    states, adjoints, ending, new_start, back, landed, products, grad_parts, side, coefs,
    adj_send, adj_recv, state_send, state_recv, cross_send, cross_recv,
    back_send, back_recv, grad_send, grad_recv,
):
    n, slices, strip, rows, cols, width, share = geo
    own_tiles = width // LANES
    tiles = own_tiles + 1
    span = tiles * LANES
    lead = rows // 8
    workers = n // share
    me = lax.axis_index("space")
    cut = lax.axis_index("cuts")
    my_worker = me // share
    last = cut == slices - 1

    barrier = pltpu.get_barrier_semaphore()
    partners = [(a, b) for b in range(slices) for a in range(n) if (a, b) != (0, 0)]
    for a, b in partners:
        pl.semaphore_signal(
            barrier, inc=1,
            device_id={"space": lax.rem(me + a, n), "cuts": lax.rem(cut + b, slices)},
            device_id_type=MESH,
        )

    lane = lax.broadcasted_iota(jnp.int32, (8, LANES), 1)
    sub = lax.broadcasted_iota(jnp.int32, (8, LANES), 0)

    def fields_of(ref, start):
        return ref[:, :, pl.ds(pl.multiple_of(start, LANES), LANES)]

    def pack(target, ref, worker, with_depth):
        first = worker * width
        after = jnp.minimum(first + width, cols - LANES)
        before = jnp.maximum(first - LANES, 0)
        right_in = worker < workers - 1
        left_in = worker > 0
        low = lane < HALF
        for t in range(own_tiles):
            target[pl.ds(0, 3), t] = fields_of(ref, first + t * LANES)
        right = jnp.where(right_in, fields_of(ref, after), 0.0)
        left = jnp.where(left_in, fields_of(ref, before), 0.0)
        target[pl.ds(0, 3), own_tiles] = jnp.where(low, right, left)
        if with_depth:
            def depth_at(start):
                at = pl.ds(pl.multiple_of(start, LANES), LANES)
                return depth_ref[:, at].astype(jnp.float32)

            for t in range(own_tiles):
                target[3, t] = depth_at(first + t * LANES)
            target[3, own_tiles] = jnp.where(low, depth_at(after), depth_at(before))

    my_rows = pl.ds(pl.multiple_of(me * strip, strip), strip)

    def outward(buffer, landing, sends, receives, k):
        return pltpu.make_async_remote_copy(
            src_ref=buffer.at[k],
            dst_ref=landing.at[:, :, my_rows, :],
            send_sem=sends.at[k],
            recv_sem=receives.at[k],
            device_id={"space": lax.rem(me + k, n)},
            device_id_type=MESH,
        )

    for k in range(1, n):
        pack(send_adj.at[k], adjoint_ref, lax.rem(me + k, n) // share, True)
    pl.semaphore_wait(barrier, len(partners))
    for k in range(1, n):
        outward(send_adj, recv_adj, adj_send, adj_recv, k).start()
    for k in range(1, n):
        pack(send_state.at[k], state_ref, lax.rem(me + k, n) // share, False)
        outward(send_state, recv_state, state_send, state_recv, k).start()
    pack(recv_adj.at[:, :, my_rows, :], adjoint_ref, my_worker, True)
    pack(recv_state.at[:, :, my_rows, :], state_ref, my_worker, False)

    total = jnp.where(last, counts_ref[slices - 1], counts_ref[0])
    for s in range(1, slices - 1):
        total = jnp.where(cut == s, counts_ref[s], total)
    coarse_rate = total.astype(jnp.float32) * fine_rate

    def fold(k, o, c, sign):
        if k == 4:
            return 0.0
        if o == 0 and c != 0 or c == 0 and o != 0:
            field = o + c
            side_of = {5: (1, 1), 3: (1, -1), 7: (2, 1), 1: (2, -1)}.get(k)
            if side_of is not None and side_of[0] == field:
                if (sign < 0) == (c == 0):
                    return sign * side_of[1] * 0.5
        return 0.0

    for k in range(9):
        for o in range(3):
            for c in range(3):
                at = (k * 3 + o) * 3 + c
                one = 1.0 if k == 4 and o == c else 0.0
                forward = weights_ref[k, o, c] + fold(k, o, c, -1.0)
                backward = weights_ref[8 - k, c, o] + fold(k, o, c, 1.0)
                coefs[0, at] = one + fine_rate * forward
                coefs[1, at] = one + fine_rate * backward
                coefs[2, at] = one + coarse_rate * backward

    lane_wide = lax.broadcasted_iota(jnp.int32, (8, span), 1) - width
    in_left = (lane_wide >= HALF) & (my_worker == 0)
    in_right = (lane_wide >= 0) & (lane_wide < HALF) & (my_worker == workers - 1)
    inside = jnp.where(in_left | in_right, 0.0, 1.0)
    side[...] = inside

    sub_wide = lax.broadcasted_iota(jnp.int32, (8, span), 0)

    def wrap(ref):
        for c in range(ref.shape[0]):
            ref[c, 0] = jnp.where(sub_wide == 0, 0.0, pltpu.roll(ref[c, lead], 1, 0))
            ref[c, lead + 1] = jnp.where(sub_wide == 7, 0.0, pltpu.roll(ref[c, 1], 7, 0))

    def arrive(landing, field, i):
        return [landing[field, t, pl.ds(i, 8, stride=lead), :] for t in range(tiles)]

    def spread(landing, target):
        def row(i, carry):
            for c in range(3):
                for t, tile in enumerate(arrive(landing, c, i)):
                    target[c, i + 1, :, t * LANES:(t + 1) * LANES] = tile
            return carry

        lax.fori_loop(0, lead, row, 0)
        wrap(target)

    for k in range(1, n):
        outward(send_adj, recv_adj, adj_send, adj_recv, k).wait_recv()
    spread(recv_adj, adjoints.at[FINE])

    def coefficient_row(i, carry):
        for t, kind in enumerate(arrive(recv_adj, 3, i)):
            depth = jnp.full((8, LANES), table_ref[0, 0], jnp.float32)
            drag = jnp.full((8, LANES), table_ref[1, 0], jnp.float32)
            for j in range(1, table_ref.shape[1]):
                same = kind == float(j)
                depth = jnp.where(same, table_ref[0, j], depth)
                drag = jnp.where(same, table_ref[1, j], drag)
            depth_half[0, i + 1, :, t * LANES:(t + 1) * LANES] = 0.5 * depth
            friction[i, :, t * LANES:(t + 1) * LANES] = drag
        return carry

    lax.fori_loop(0, lead, coefficient_row, 0)
    wrap(depth_half)

    def shift_row(i, carry):
        here = depth_half[0, i + 1]
        depth_east[i] = pltpu.roll(here, span - 1, 1)
        depth_west[i] = pltpu.roll(here, 1, 1)
        return carry

    lax.fori_loop(0, lead, shift_row, 0)

    def stencil(load, which, rate, transposed, i):
        acc = [None, None, None]
        rim = {}
        for c in range(3):
            x = load(c, pl.ds(i, BLOCK + 2))
            moved = (pltpu.roll(x, 1, 2), x, pltpu.roll(x, span - 1, 2))
            for dc in range(3):
                for dr in range(3):
                    view = moved[dc][dr:dr + BLOCK]
                    rim[c, dr, dc] = view
                    for o in range(3):
                        term = coefs[which, ((3 * dr + dc) * 3 + o) * 3 + c] * view
                        acc[o] = term if acc[o] is None else acc[o] + term
            drag = rate * friction[pl.ds(i, BLOCK)]
            if c:
                acc[c] = acc[c] - drag * rim[c, 1, 1]
            if transposed and c == 0:
                here = pl.ds(i, BLOCK)
                acc[1] = acc[1] + rate * (
                    depth_east[here] * rim[0, 1, 2] - depth_west[here] * rim[0, 1, 0]
                )
                acc[2] = acc[2] + rate * (
                    depth_half[0, pl.ds(i + 2, BLOCK)] * rim[0, 2, 1]
                    - depth_half[0, pl.ds(i, BLOCK)] * rim[0, 0, 1]
                )
        if not transposed:
            slope = (rim[1, 1, 2] - rim[1, 1, 0]) + (rim[2, 2, 1] - rim[2, 0, 1])
            acc[0] = acc[0] - rate * (depth_half[0, pl.ds(i + 1, BLOCK)] * slope)
        return [a * side[...] for a in acc]

    blocks = lead // BLOCK

    def adjoint_step(turn, carry):
        step = FINE - 1 - turn
        active = step < total

        def one(b, inner):
            i = b * BLOCK
            found = stencil(lambda c, at: adjoints[step + 1, c, at], 1, fine_rate, True, i)
            for c in range(3):
                old = adjoints[step + 1, c, pl.ds(i + 1, BLOCK)]
                adjoints[step, c, pl.ds(i + 1, BLOCK)] = jnp.where(active, found[c], old)
            return inner

        lax.fori_loop(0, blocks, one, 0)
        wrap(adjoints.at[step])
        return carry

    lax.fori_loop(0, FINE, adjoint_step, 0)

    def homeward(k):
        target = lax.rem(me + k, n)
        return pltpu.make_async_remote_copy(
            src_ref=back.at[:, :, pl.ds(pl.multiple_of(target * strip, strip), strip), :],
            dst_ref=landed.at[:, pl.ds(my_worker * own_tiles, own_tiles), :, :],
            send_sem=back_send.at[k],
            recv_sem=back_recv.at[k],
            device_id={"space": target},
            device_id_type=MESH,
        )

    def leads(device):
        return lax.rem(device, share) == 0

    def when(condition):
        return pl.when(condition) if share > 1 else (lambda f: f())

    def correct():
        for c in range(3):
            def change(i, carry):
                ending[c, i] = ending[c, i] - adjoints[FINE, c, i]
                return carry

            lax.fori_loop(0, lead + 2, change, 0)

        def one(b, carry):
            i = b * BLOCK
            found = stencil(lambda c, at: ending[c, at], 2, coarse_rate, True, i)
            for c in range(3):
                new_start[c, pl.ds(i + 1, BLOCK)] = (
                    found[c] + adjoints[0, c, pl.ds(i + 1, BLOCK)]
                )
            return carry

        lax.fori_loop(0, blocks, one, 0)
        wrap(new_start)

    def go_home():
        def row(i, carry):
            for c in range(3):
                for t in range(own_tiles):
                    back[c, t, pl.ds(i, 8, stride=lead), :] = new_start[
                        c, i + 1, :, t * LANES:(t + 1) * LANES
                    ]
            return carry

        lax.fori_loop(0, lead, row, 0)

        @when(leads(me))
        def _():
            for k in range(1, n):
                homeward(k).start()
            landed[:, pl.ds(my_worker * own_tiles, own_tiles)] = back[:, :, my_rows, :]

    def across():
        return pltpu.make_async_remote_copy(
            src_ref=new_start,
            dst_ref=ending,
            send_sem=cross_send,
            recv_sem=cross_recv,
            device_id={"cuts": lax.rem(cut + slices - 1, slices)},
            device_id_type=MESH,
        )

    @pl.when(last)
    def _():
        for c in range(3):
            def change(i, carry):
                ending[c, i] = adjoints[FINE, c, i]
                return carry

            lax.fori_loop(0, lead + 2, change, 0)
        correct()
        if slices > 1:
            across().start()
        go_home()

    for k in range(1, n):
        outward(send_state, recv_state, state_send, state_recv, k).wait_recv()
    spread(recv_state, states.at[0])

    def forward_step(step, carry):
        def one(b, inner):
            i = b * BLOCK
            found = stencil(lambda c, at: states[step, c, at], 0, fine_rate, False, i)
            for c in range(3):
                states[step + 1, c, pl.ds(i + 1, BLOCK)] = found[c]
            return inner

        lax.fori_loop(0, blocks, one, 0)
        wrap(states.at[step + 1])
        return carry

    lax.fori_loop(0, FINE - 1, forward_step, 0)

    if slices > 1:
        @pl.when(jnp.logical_not(last))
        def _():
            across().wait_recv()
            correct()
            go_home()

            @pl.when(cut > 0)
            def _():
                across().start()

    grad_scale = fine_rate * float(rows * cols * slices) ** (-0.5) / share
    zero = jnp.zeros((8, LANES), jnp.float32)
    own = own_tiles * LANES

    for c in range(3):
        def pairs(turn, sums):
            step = turn // (lead // GRAD_BLOCK)
            i = (turn % (lead // GRAD_BLOCK)) * GRAD_BLOCK
            factor = jnp.where(step < total, grad_scale, 0.0)
            x = states[step, c, pl.ds(i, GRAD_BLOCK + 2)]
            lam = [
                factor * adjoints[step + 1, o, pl.ds(i + 1, GRAD_BLOCK), :, 0:own]
                for o in range(3)
            ]
            moved = (pltpu.roll(x, 1, 2), x, pltpu.roll(x, span - 1, 2))
            result = []
            for dr in range(3):
                for dc in range(3):
                    view = moved[dc][dr:dr + GRAD_BLOCK, :, 0:own]
                    for o in range(3):
                        prod = view * lam[o]
                        part = sums[len(result)]
                        for r in range(GRAD_BLOCK):
                            for t in range(own_tiles):
                                part = part + prod[r, :, t * LANES:(t + 1) * LANES]
                        result.append(part)
            return tuple(result)

        sums = lax.fori_loop(0, FINE * (lead // GRAD_BLOCK), pairs, (zero,) * 27)
        for at in range(27):
            products[at * 3 + c] = sums[at]
    for at in range(81, products.shape[0]):
        products[at] = zero

    column = jnp.sum(jnp.sum(products[...], axis=1), axis=1, keepdims=True)
    count = products.shape[0]
    diagonal = lax.broadcasted_iota(jnp.int32, (count, LANES), 0) == lax.broadcasted_iota(
        jnp.int32, (count, LANES), 1
    )
    line = jnp.sum(jnp.where(diagonal, column, 0.0), axis=0, keepdims=True)
    grad_parts[0] = jnp.broadcast_to(line, (8, LANES))

    def share_grad(j):
        a, b = partners[j]
        return pltpu.make_async_remote_copy(
            src_ref=grad_parts.at[0],
            dst_ref=grad_parts.at[j + 1],
            send_sem=grad_send.at[j],
            recv_sem=grad_recv.at[j],
            device_id={"space": lax.rem(me + a, n), "cuts": lax.rem(cut + b, slices)},
            device_id_type=MESH,
        )

    for j in range(len(partners)):
        share_grad(j).start()

    for k in range(1, n):
        @when(leads(lax.rem(me + n - k, n)))
        def _():
            homeward(k).wait_recv()

    for t in range(cols // LANES):
        out_ref[0, :, :, t * LANES:(t + 1) * LANES] = landed[:, t]

    whole = grad_parts[0]
    for j in range(len(partners)):
        share_grad(j).wait_recv()
        whole = whole + grad_parts[j + 1]
    grad_ref[...] = whole

    for k in range(1, n):
        outward(send_adj, recv_adj, adj_send, adj_recv, k).wait_send()
        outward(send_state, recv_state, state_send, state_recv, k).wait_send()

    @when(leads(me))
    def _():
        for k in range(1, n):
            homeward(k).wait_send()

    if slices > 1:
        @pl.when(cut > 0)
        def _():
            across().wait_send()

    for j in range(len(partners)):
        share_grad(j).wait_send()


def body(depth_class, coef_table, step_counts, closure_weights, checkpoints, old_adjoint):
    n = lax.axis_size("space")
    slices = lax.axis_size("cuts")
    strip, cols = depth_class.shape
    rows = strip * n
    width = max(cols // n, LANES)
    share = width * n // cols
    tiles = width // LANES + 1
    span = tiles * LANES
    lead = rows // 8
    geo = (n, slices, strip, rows, cols, width, share)
    partners = n * slices - 1
    f32 = jnp.float32
    vmem = pl.BlockSpec(memory_space=pltpu.VMEM)
    smem = pl.BlockSpec(memory_space=pltpu.SMEM)
    dma = pltpu.SemaphoreType.DMA
    new_adjoint, grad = pl.pallas_call(
        functools.partial(kernel, geo),
        out_shape=(
            jax.ShapeDtypeStruct((1, 3, strip, cols), f32),
            jax.ShapeDtypeStruct((8, LANES), f32),
        ),
        in_specs=[vmem, smem, smem, smem, vmem, vmem],
        out_specs=(vmem, vmem),
        scratch_shapes=[
            pltpu.VMEM((n, 4, tiles, strip, LANES), f32),
            pltpu.VMEM((n, 3, tiles, strip, LANES), f32),
            pltpu.VMEM((4, tiles, rows, LANES), f32),
            pltpu.VMEM((3, tiles, rows, LANES), f32),
            pltpu.VMEM((1, lead + 2, 8, span), f32),
            pltpu.VMEM((lead, 8, span), f32),
            pltpu.VMEM((lead, 8, span), f32),
            pltpu.VMEM((lead, 8, span), f32),
            pltpu.VMEM((FINE, 3, lead + 2, 8, span), f32),
            pltpu.VMEM((FINE + 1, 3, lead + 2, 8, span), f32),
            pltpu.VMEM((3, lead + 2, 8, span), f32),
            pltpu.VMEM((3, lead + 2, 8, span), f32),
            pltpu.VMEM((3, tiles - 1, rows, LANES), f32),
            pltpu.VMEM((3, cols // LANES, strip, LANES), f32),
            pltpu.VMEM((88, 8, LANES), f32),
            pltpu.VMEM((partners + 1, 8, LANES), f32),
            pltpu.VMEM((8, span), f32),
            pltpu.SMEM((3, 81), f32),
            dma((n,)), dma((n,)), dma((n,)), dma((n,)),
            dma(()), dma(()),
            dma((n,)), dma((n,)),
            dma((partners,)), dma((partners,)),
        ],
        compiler_params=pltpu.CompilerParams(
            collective_id=0, has_side_effects=True, vmem_limit_bytes=48 * 1024 * 1024
        ),
    )(depth_class, coef_table, step_counts, closure_weights, checkpoints[0], old_adjoint[0])
    return new_adjoint, grad[0, :81].reshape(9, 3, 3)


def solution(mesh):
    return jax.shard_map(
        body,
        mesh=mesh,
        in_specs=(
            P("space", None),
            P(),
            P(),
            P("member", None, None),
            P(("member", "cuts"), None, "space", None),
            P(("member", "cuts"), None, "space", None),
        ),
        out_specs=(P(("member", "cuts"), None, "space", None), P("member", None, None)),
        check_vma=False,
    )
```

```python
import functools

import jax
import jax.numpy as jnp
from jax import lax
from jax.experimental import pallas as pl
from jax.experimental.pallas import tpu as pltpu
from jax.sharding import PartitionSpec as P

FINE = 12
fine_rate = 0.05
LANES = 128
HALF = LANES // 2
RIM = 16
MESH = pl.DeviceIdType.MESH
BLOCK = 4
GRAD_BLOCK = 8


def kernel(
    geo,
    depth_ref, table_ref, counts_ref, weights_ref, state_ref, adjoint_ref,
    out_ref, grad_ref,
    send_adj, send_state, recv_adj, recv_state, depth_half, depth_east, depth_west, friction,
    states, adjoints, ending, new_start, back, landed, products, grad_parts, side, coefs,
    adj_send, adj_recv, state_send, state_recv, cross_send, cross_recv,
    back_send, back_recv, grad_send, grad_recv,
):
    n, slices, strip, rows, cols, width, share = geo
    own_tiles = width // LANES
    tiles = own_tiles + 1
    span = tiles * LANES
    lead = rows // 8
    workers = n // share
    me = lax.axis_index("space")
    cut = lax.axis_index("cuts")
    my_worker = me // share
    last = cut == slices - 1

    barrier = pltpu.get_barrier_semaphore()
    partners = [(a, b) for b in range(slices) for a in range(n) if (a, b) != (0, 0)]
    for a, b in partners:
        pl.semaphore_signal(
            barrier, inc=1,
            device_id={"space": lax.rem(me + a, n), "cuts": lax.rem(cut + b, slices)},
            device_id_type=MESH,
        )

    lane = lax.broadcasted_iota(jnp.int32, (8, LANES), 1)
    sub = lax.broadcasted_iota(jnp.int32, (8, LANES), 0)

    def pack(target, ref, worker, with_depth):
        first = worker * width
        after = jnp.minimum(first + width, cols - LANES)
        before = jnp.maximum(first - LANES, 0)
        right_in = worker < workers - 1
        left_in = worker > 0
        def depth_at(start):
            at = pl.ds(pl.multiple_of(start, LANES), LANES)
            return depth_ref[:, at].astype(jnp.float32)

        def tile_at(f, start):
            if f == 3:
                return depth_at(start)
            return ref[f, :, pl.ds(pl.multiple_of(start, LANES), LANES)]

        count = 4 if with_depth else 3
        rims = None
        for f in range(count):
            for t in range(own_tiles):
                target[f * own_tiles + t] = tile_at(f, first + t * LANES)
            right = jnp.where(right_in, tile_at(f, after), 0.0)
            left = jnp.where(left_in, tile_at(f, before), 0.0)
            both = pltpu.roll(jnp.where(lane < HALF, right, left), (2 * f + 1) * RIM % LANES, 1)
            rims = both if rims is None else jnp.where(lane < 2 * RIM * f, rims, both)
        target[count * own_tiles] = rims

    my_rows = pl.ds(pl.multiple_of(me * strip, strip), strip)

    def outward(buffer, landing, sends, receives, k):
        return pltpu.make_async_remote_copy(
            src_ref=buffer.at[k],
            dst_ref=landing.at[:, my_rows, :],
            send_sem=sends.at[k],
            recv_sem=receives.at[k],
            device_id={"space": lax.rem(me + k, n)},
            device_id_type=MESH,
        )

    for k in range(1, n):
        pack(send_adj.at[k], adjoint_ref, lax.rem(me + k, n) // share, True)
    pl.semaphore_wait(barrier, len(partners))
    for k in range(1, n):
        outward(send_adj, recv_adj, adj_send, adj_recv, k).start()
    for k in range(1, n):
        pack(send_state.at[k], state_ref, lax.rem(me + k, n) // share, False)
        outward(send_state, recv_state, state_send, state_recv, k).start()
    pack(recv_adj.at[:, my_rows, :], adjoint_ref, my_worker, True)
    pack(recv_state.at[:, my_rows, :], state_ref, my_worker, False)

    total = jnp.where(last, counts_ref[slices - 1], counts_ref[0])
    for s in range(1, slices - 1):
        total = jnp.where(cut == s, counts_ref[s], total)
    coarse_rate = total.astype(jnp.float32) * fine_rate

    def fold(k, o, c, sign):
        if k == 4:
            return 0.0
        if o == 0 and c != 0 or c == 0 and o != 0:
            field = o + c
            side_of = {5: (1, 1), 3: (1, -1), 7: (2, 1), 1: (2, -1)}.get(k)
            if side_of is not None and side_of[0] == field:
                if (sign < 0) == (c == 0):
                    return sign * side_of[1] * 0.5
        return 0.0

    for k in range(9):
        for o in range(3):
            for c in range(3):
                at = (k * 3 + o) * 3 + c
                one = 1.0 if k == 4 and o == c else 0.0
                forward = weights_ref[k, o, c] + fold(k, o, c, -1.0)
                backward = weights_ref[8 - k, c, o] + fold(k, o, c, 1.0)
                coefs[0, at] = one + fine_rate * forward
                coefs[1, at] = one + fine_rate * backward
                coefs[2, at] = one + coarse_rate * backward

    lane_wide = lax.broadcasted_iota(jnp.int32, (8, span), 1) - width
    in_left = (lane_wide >= HALF) & (my_worker == 0)
    in_right = (lane_wide >= 0) & (lane_wide < HALF) & (my_worker == workers - 1)
    inside = jnp.where(in_left | in_right, 0.0, 1.0)
    side[...] = inside

    sub_wide = lax.broadcasted_iota(jnp.int32, (8, span), 0)

    def wrap(ref):
        for c in range(ref.shape[0]):
            ref[c, 0] = jnp.where(sub_wide == 0, 0.0, pltpu.roll(ref[c, lead], 1, 0))
            ref[c, lead + 1] = jnp.where(sub_wide == 7, 0.0, pltpu.roll(ref[c, 1], 7, 0))

    def arrive(landing, field, i):
        at = pl.ds(i, 8, stride=lead)
        found = [landing[field * own_tiles + t, at, :] for t in range(own_tiles)]
        rims = landing[landing.shape[0] - 1, at, :]
        rims = pltpu.roll(rims, (LANES - (2 * field + 1) * RIM) % LANES, 1)
        near = (lane < RIM) | (lane >= LANES - RIM)
        return found + [jnp.where(near, rims, 0.0)]

    def spread(landing, target):
        def row(i, carry):
            for c in range(3):
                for t, tile in enumerate(arrive(landing, c, i)):
                    target[c, i + 1, :, t * LANES:(t + 1) * LANES] = tile
            return carry

        lax.fori_loop(0, lead, row, 0)
        wrap(target)

    for k in range(1, n):
        outward(send_adj, recv_adj, adj_send, adj_recv, k).wait_recv()
    spread(recv_adj, adjoints.at[FINE])

    def coefficient_row(i, carry):
        for t, kind in enumerate(arrive(recv_adj, 3, i)):
            depth = jnp.full((8, LANES), table_ref[0, 0], jnp.float32)
            drag = jnp.full((8, LANES), table_ref[1, 0], jnp.float32)
            for j in range(1, table_ref.shape[1]):
                same = kind == float(j)
                depth = jnp.where(same, table_ref[0, j], depth)
                drag = jnp.where(same, table_ref[1, j], drag)
            depth_half[0, i + 1, :, t * LANES:(t + 1) * LANES] = 0.5 * depth
            friction[i, :, t * LANES:(t + 1) * LANES] = drag
        return carry

    lax.fori_loop(0, lead, coefficient_row, 0)
    wrap(depth_half)

    def shift_row(i, carry):
        here = depth_half[0, i + 1]
        depth_east[i] = pltpu.roll(here, span - 1, 1)
        depth_west[i] = pltpu.roll(here, 1, 1)
        return carry

    lax.fori_loop(0, lead, shift_row, 0)

    def stencil(load, which, rate, transposed, i):
        acc = [None, None, None]
        rim = {}
        for c in range(3):
            x = load(c, pl.ds(i, BLOCK + 2))
            moved = (pltpu.roll(x, 1, 2), x, pltpu.roll(x, span - 1, 2))
            for dc in range(3):
                for dr in range(3):
                    view = moved[dc][dr:dr + BLOCK]
                    rim[c, dr, dc] = view
                    for o in range(3):
                        term = coefs[which, ((3 * dr + dc) * 3 + o) * 3 + c] * view
                        acc[o] = term if acc[o] is None else acc[o] + term
            drag = rate * friction[pl.ds(i, BLOCK)]
            if c:
                acc[c] = acc[c] - drag * rim[c, 1, 1]
            if transposed and c == 0:
                here = pl.ds(i, BLOCK)
                acc[1] = acc[1] + rate * (
                    depth_east[here] * rim[0, 1, 2] - depth_west[here] * rim[0, 1, 0]
                )
                acc[2] = acc[2] + rate * (
                    depth_half[0, pl.ds(i + 2, BLOCK)] * rim[0, 2, 1]
                    - depth_half[0, pl.ds(i, BLOCK)] * rim[0, 0, 1]
                )
        if not transposed:
            slope = (rim[1, 1, 2] - rim[1, 1, 0]) + (rim[2, 2, 1] - rim[2, 0, 1])
            acc[0] = acc[0] - rate * (depth_half[0, pl.ds(i + 1, BLOCK)] * slope)
        return [a * side[...] for a in acc]

    blocks = lead // BLOCK

    def adjoint_step(turn, carry):
        step = FINE - 1 - turn
        active = step < total

        def one(b, inner):
            i = b * BLOCK
            found = stencil(lambda c, at: adjoints[step + 1, c, at], 1, fine_rate, True, i)
            for c in range(3):
                old = adjoints[step + 1, c, pl.ds(i + 1, BLOCK)]
                adjoints[step, c, pl.ds(i + 1, BLOCK)] = jnp.where(active, found[c], old)
            return inner

        lax.fori_loop(0, blocks, one, 0)
        wrap(adjoints.at[step])
        return carry

    lax.fori_loop(0, FINE, adjoint_step, 0)

    def homeward(k):
        target = lax.rem(me + k, n)
        return pltpu.make_async_remote_copy(
            src_ref=back.at[:, :, pl.ds(pl.multiple_of(target * strip, strip), strip), :],
            dst_ref=landed.at[:, pl.ds(my_worker * own_tiles, own_tiles), :, :],
            send_sem=back_send.at[k],
            recv_sem=back_recv.at[k],
            device_id={"space": target},
            device_id_type=MESH,
        )

    def leads(device):
        return lax.rem(device, share) == 0

    def when(condition):
        return pl.when(condition) if share > 1 else (lambda f: f())

    def correct():
        for c in range(3):
            def change(i, carry):
                ending[c, i] = ending[c, i] - adjoints[FINE, c, i]
                return carry

            lax.fori_loop(0, lead + 2, change, 0)

        def one(b, carry):
            i = b * BLOCK
            found = stencil(lambda c, at: ending[c, at], 2, coarse_rate, True, i)
            for c in range(3):
                new_start[c, pl.ds(i + 1, BLOCK)] = (
                    found[c] + adjoints[0, c, pl.ds(i + 1, BLOCK)]
                )
            return carry

        lax.fori_loop(0, blocks, one, 0)
        wrap(new_start)

    def go_home():
        def row(i, carry):
            for c in range(3):
                for t in range(own_tiles):
                    back[c, t, pl.ds(i, 8, stride=lead), :] = new_start[
                        c, i + 1, :, t * LANES:(t + 1) * LANES
                    ]
            return carry

        lax.fori_loop(0, lead, row, 0)

        @when(leads(me))
        def _():
            for k in range(1, n):
                homeward(k).start()
            landed[:, pl.ds(my_worker * own_tiles, own_tiles)] = back[:, :, my_rows, :]

    def across():
        return pltpu.make_async_remote_copy(
            src_ref=new_start,
            dst_ref=ending,
            send_sem=cross_send,
            recv_sem=cross_recv,
            device_id={"cuts": lax.rem(cut + slices - 1, slices)},
            device_id_type=MESH,
        )

    @pl.when(last)
    def _():
        for c in range(3):
            def change(i, carry):
                ending[c, i] = adjoints[FINE, c, i]
                return carry

            lax.fori_loop(0, lead + 2, change, 0)
        correct()
        if slices > 1:
            across().start()
        go_home()

    for k in range(1, n):
        outward(send_state, recv_state, state_send, state_recv, k).wait_recv()
    spread(recv_state, states.at[0])

    def forward_step(step, carry):
        def one(b, inner):
            i = b * BLOCK
            found = stencil(lambda c, at: states[step, c, at], 0, fine_rate, False, i)
            for c in range(3):
                states[step + 1, c, pl.ds(i + 1, BLOCK)] = found[c]
            return inner

        lax.fori_loop(0, blocks, one, 0)
        wrap(states.at[step + 1])
        return carry

    lax.fori_loop(0, FINE - 1, forward_step, 0)

    if slices > 1:
        @pl.when(jnp.logical_not(last))
        def _():
            across().wait_recv()
            correct()
            go_home()

            @pl.when(cut > 0)
            def _():
                across().start()

    grad_scale = fine_rate * float(rows * cols * slices) ** (-0.5) / share
    zero = jnp.zeros((8, LANES), jnp.float32)
    own = own_tiles * LANES

    for c in range(3):
        def pairs(turn, sums):
            step = turn // (lead // GRAD_BLOCK)
            i = (turn % (lead // GRAD_BLOCK)) * GRAD_BLOCK
            factor = jnp.where(step < total, grad_scale, 0.0)
            x = states[step, c, pl.ds(i, GRAD_BLOCK + 2)]
            lam = [
                factor * adjoints[step + 1, o, pl.ds(i + 1, GRAD_BLOCK), :, 0:own]
                for o in range(3)
            ]
            moved = (pltpu.roll(x, 1, 2), x, pltpu.roll(x, span - 1, 2))
            result = []
            for dr in range(3):
                for dc in range(3):
                    view = moved[dc][dr:dr + GRAD_BLOCK, :, 0:own]
                    for o in range(3):
                        prod = view * lam[o]
                        part = sums[len(result)]
                        for r in range(GRAD_BLOCK):
                            for t in range(own_tiles):
                                part = part + prod[r, :, t * LANES:(t + 1) * LANES]
                        result.append(part)
            return tuple(result)

        sums = lax.fori_loop(0, FINE * (lead // GRAD_BLOCK), pairs, (zero,) * 27)
        for at in range(27):
            products[at * 3 + c] = sums[at]
    for at in range(81, products.shape[0]):
        products[at] = zero

    column = jnp.sum(jnp.sum(products[...], axis=1), axis=1, keepdims=True)
    count = products.shape[0]
    diagonal = lax.broadcasted_iota(jnp.int32, (count, LANES), 0) == lax.broadcasted_iota(
        jnp.int32, (count, LANES), 1
    )
    line = jnp.sum(jnp.where(diagonal, column, 0.0), axis=0, keepdims=True)
    grad_parts[0] = jnp.broadcast_to(line, (8, LANES))

    def share_grad(j):
        a, b = partners[j]
        return pltpu.make_async_remote_copy(
            src_ref=grad_parts.at[0],
            dst_ref=grad_parts.at[j + 1],
            send_sem=grad_send.at[j],
            recv_sem=grad_recv.at[j],
            device_id={"space": lax.rem(me + a, n), "cuts": lax.rem(cut + b, slices)},
            device_id_type=MESH,
        )

    for j in range(len(partners)):
        share_grad(j).start()

    for k in range(1, n):
        @when(leads(lax.rem(me + n - k, n)))
        def _():
            homeward(k).wait_recv()

    for t in range(cols // LANES):
        out_ref[0, :, :, t * LANES:(t + 1) * LANES] = landed[:, t]

    whole = grad_parts[0]
    for j in range(len(partners)):
        share_grad(j).wait_recv()
        whole = whole + grad_parts[j + 1]
    grad_ref[...] = whole

    for k in range(1, n):
        outward(send_adj, recv_adj, adj_send, adj_recv, k).wait_send()
        outward(send_state, recv_state, state_send, state_recv, k).wait_send()

    @when(leads(me))
    def _():
        for k in range(1, n):
            homeward(k).wait_send()

    if slices > 1:
        @pl.when(cut > 0)
        def _():
            across().wait_send()

    for j in range(len(partners)):
        share_grad(j).wait_send()


def body(depth_class, coef_table, step_counts, closure_weights, checkpoints, old_adjoint):
    n = lax.axis_size("space")
    slices = lax.axis_size("cuts")
    strip, cols = depth_class.shape
    rows = strip * n
    width = max(cols // n, LANES)
    share = width * n // cols
    tiles = width // LANES + 1
    span = tiles * LANES
    lead = rows // 8
    geo = (n, slices, strip, rows, cols, width, share)
    partners = n * slices - 1
    f32 = jnp.float32
    vmem = pl.BlockSpec(memory_space=pltpu.VMEM)
    smem = pl.BlockSpec(memory_space=pltpu.SMEM)
    dma = pltpu.SemaphoreType.DMA
    new_adjoint, grad = pl.pallas_call(
        functools.partial(kernel, geo),
        out_shape=(
            jax.ShapeDtypeStruct((1, 3, strip, cols), f32),
            jax.ShapeDtypeStruct((8, LANES), f32),
        ),
        in_specs=[vmem, smem, smem, smem, vmem, vmem],
        out_specs=(vmem, vmem),
        scratch_shapes=[
            pltpu.VMEM((n, 4 * tiles - 3, strip, LANES), f32),
            pltpu.VMEM((n, 3 * tiles - 2, strip, LANES), f32),
            pltpu.VMEM((4 * tiles - 3, rows, LANES), f32),
            pltpu.VMEM((3 * tiles - 2, rows, LANES), f32),
            pltpu.VMEM((1, lead + 2, 8, span), f32),
            pltpu.VMEM((lead, 8, span), f32),
            pltpu.VMEM((lead, 8, span), f32),
            pltpu.VMEM((lead, 8, span), f32),
            pltpu.VMEM((FINE, 3, lead + 2, 8, span), f32),
            pltpu.VMEM((FINE + 1, 3, lead + 2, 8, span), f32),
            pltpu.VMEM((3, lead + 2, 8, span), f32),
            pltpu.VMEM((3, lead + 2, 8, span), f32),
            pltpu.VMEM((3, tiles - 1, rows, LANES), f32),
            pltpu.VMEM((3, cols // LANES, strip, LANES), f32),
            pltpu.VMEM((88, 8, LANES), f32),
            pltpu.VMEM((partners + 1, 8, LANES), f32),
            pltpu.VMEM((8, span), f32),
            pltpu.SMEM((3, 81), f32),
            dma((n,)), dma((n,)), dma((n,)), dma((n,)),
            dma(()), dma(()),
            dma((n,)), dma((n,)),
            dma((partners,)), dma((partners,)),
        ],
        compiler_params=pltpu.CompilerParams(
            collective_id=0, has_side_effects=True, vmem_limit_bytes=48 * 1024 * 1024
        ),
    )(depth_class, coef_table, step_counts, closure_weights, checkpoints[0], old_adjoint[0])
    return new_adjoint, grad[0, :81].reshape(9, 3, 3)


def solution(mesh):
    return jax.shard_map(
        body,
        mesh=mesh,
        in_specs=(
            P("space", None),
            P(),
            P(),
            P("member", None, None),
            P(("member", "cuts"), None, "space", None),
            P(("member", "cuts"), None, "space", None),
        ),
        out_specs=(P(("member", "cuts"), None, "space", None), P("member", None, None)),
        check_vma=False,
    )
```

```python
import functools

import jax
import jax.numpy as jnp
from jax import lax
from jax.experimental import pallas as pl
from jax.experimental.pallas import tpu as pltpu
from jax.sharding import PartitionSpec as P

FINE = 12
fine_rate = 0.05
LANES = 128
HALF = LANES // 2
RIM = 16
MESH = pl.DeviceIdType.MESH
BLOCK = 8
GRAD_BLOCK = 8


def kernel(
    geo,
    depth_ref, table_ref, counts_ref, weights_ref, state_ref, adjoint_ref,
    out_ref, grad_ref,
    send_adj, send_state, recv_adj, recv_state, depth_half, depth_east, depth_west, friction,
    states, adjoints, ending, new_start, back, landed, products, grad_parts, side, coefs,
    adj_send, adj_recv, state_send, state_recv, cross_send, cross_recv,
    back_send, back_recv, grad_send, grad_recv,
):
    n, slices, strip, rows, cols, width, share = geo
    own_tiles = width // LANES
    tiles = own_tiles + 1
    span = tiles * LANES
    lead = rows // 8
    workers = n // share
    me = lax.axis_index("space")
    cut = lax.axis_index("cuts")
    my_worker = me // share
    last = cut == slices - 1

    barrier = pltpu.get_barrier_semaphore()
    partners = [(a, b) for b in range(slices) for a in range(n) if (a, b) != (0, 0)]
    for a, b in partners:
        pl.semaphore_signal(
            barrier, inc=1,
            device_id={"space": lax.rem(me + a, n), "cuts": lax.rem(cut + b, slices)},
            device_id_type=MESH,
        )

    lane = lax.broadcasted_iota(jnp.int32, (8, LANES), 1)
    sub = lax.broadcasted_iota(jnp.int32, (8, LANES), 0)

    def pack(target, ref, worker, with_depth):
        first = worker * width
        after = jnp.minimum(first + width, cols - LANES)
        before = jnp.maximum(first - LANES, 0)
        right_in = worker < workers - 1
        left_in = worker > 0
        def depth_at(start):
            at = pl.ds(pl.multiple_of(start, LANES), LANES)
            return depth_ref[:, at].astype(jnp.float32)

        def tile_at(f, start):
            if f == 3:
                return depth_at(start)
            return ref[f, :, pl.ds(pl.multiple_of(start, LANES), LANES)]

        count = 4 if with_depth else 3
        rims = None
        for f in range(count):
            for t in range(own_tiles):
                target[f * own_tiles + t] = tile_at(f, first + t * LANES)
            right = jnp.where(right_in, tile_at(f, after), 0.0)
            left = jnp.where(left_in, tile_at(f, before), 0.0)
            both = pltpu.roll(jnp.where(lane < HALF, right, left), (2 * f + 1) * RIM % LANES, 1)
            rims = both if rims is None else jnp.where(lane < 2 * RIM * f, rims, both)
        target[count * own_tiles] = rims

    my_rows = pl.ds(pl.multiple_of(me * strip, strip), strip)

    def outward(buffer, landing, sends, receives, k):
        return pltpu.make_async_remote_copy(
            src_ref=buffer.at[k],
            dst_ref=landing.at[:, my_rows, :],
            send_sem=sends.at[k],
            recv_sem=receives.at[k],
            device_id={"space": lax.rem(me + k, n)},
            device_id_type=MESH,
        )

    for k in range(1, n):
        pack(send_adj.at[k], adjoint_ref, lax.rem(me + k, n) // share, True)
    pl.semaphore_wait(barrier, len(partners))
    for k in range(1, n):
        outward(send_adj, recv_adj, adj_send, adj_recv, k).start()
    for k in range(1, n):
        pack(send_state.at[k], state_ref, lax.rem(me + k, n) // share, False)
        outward(send_state, recv_state, state_send, state_recv, k).start()
    pack(recv_adj.at[:, my_rows, :], adjoint_ref, my_worker, True)
    pack(recv_state.at[:, my_rows, :], state_ref, my_worker, False)

    total = jnp.where(last, counts_ref[slices - 1], counts_ref[0])
    for s in range(1, slices - 1):
        total = jnp.where(cut == s, counts_ref[s], total)
    coarse_rate = total.astype(jnp.float32) * fine_rate

    def fold(k, o, c, sign):
        if k == 4:
            return 0.0
        if o == 0 and c != 0 or c == 0 and o != 0:
            field = o + c
            side_of = {5: (1, 1), 3: (1, -1), 7: (2, 1), 1: (2, -1)}.get(k)
            if side_of is not None and side_of[0] == field:
                if (sign < 0) == (c == 0):
                    return sign * side_of[1] * 0.5
        return 0.0

    for k in range(9):
        for o in range(3):
            for c in range(3):
                at = (k * 3 + o) * 3 + c
                one = 1.0 if k == 4 and o == c else 0.0
                forward = weights_ref[k, o, c] + fold(k, o, c, -1.0)
                backward = weights_ref[8 - k, c, o] + fold(k, o, c, 1.0)
                coefs[0, at] = one + fine_rate * forward
                coefs[1, at] = one + fine_rate * backward
                coefs[2, at] = one + coarse_rate * backward

    lane_wide = lax.broadcasted_iota(jnp.int32, (8, span), 1) - width
    in_left = (lane_wide >= HALF) & (my_worker == 0)
    in_right = (lane_wide >= 0) & (lane_wide < HALF) & (my_worker == workers - 1)
    inside = jnp.where(in_left | in_right, 0.0, 1.0)
    side[...] = inside

    sub_wide = lax.broadcasted_iota(jnp.int32, (8, span), 0)

    def wrap(ref):
        for c in range(ref.shape[0]):
            ref[c, 0] = jnp.where(sub_wide == 0, 0.0, pltpu.roll(ref[c, lead], 1, 0))
            ref[c, lead + 1] = jnp.where(sub_wide == 7, 0.0, pltpu.roll(ref[c, 1], 7, 0))

    def arrive(landing, field, i):
        at = pl.ds(i, 8, stride=lead)
        found = [landing[field * own_tiles + t, at, :] for t in range(own_tiles)]
        rims = landing[landing.shape[0] - 1, at, :]
        rims = pltpu.roll(rims, (LANES - (2 * field + 1) * RIM) % LANES, 1)
        near = (lane < RIM) | (lane >= LANES - RIM)
        return found + [jnp.where(near, rims, 0.0)]

    def spread(landing, target):
        def row(i, carry):
            for c in range(3):
                for t, tile in enumerate(arrive(landing, c, i)):
                    target[c, i + 1, :, t * LANES:(t + 1) * LANES] = tile
            return carry

        lax.fori_loop(0, lead, row, 0)
        wrap(target)

    for k in range(1, n):
        outward(send_adj, recv_adj, adj_send, adj_recv, k).wait_recv()
    spread(recv_adj, adjoints.at[FINE])

    def coefficient_row(i, carry):
        for t, kind in enumerate(arrive(recv_adj, 3, i)):
            depth = jnp.full((8, LANES), table_ref[0, 0], jnp.float32)
            drag = jnp.full((8, LANES), table_ref[1, 0], jnp.float32)
            for j in range(1, table_ref.shape[1]):
                same = kind == float(j)
                depth = jnp.where(same, table_ref[0, j], depth)
                drag = jnp.where(same, table_ref[1, j], drag)
            depth_half[0, i + 1, :, t * LANES:(t + 1) * LANES] = 0.5 * depth
            friction[i, :, t * LANES:(t + 1) * LANES] = drag
        return carry

    lax.fori_loop(0, lead, coefficient_row, 0)
    wrap(depth_half)

    def shift_row(i, carry):
        here = depth_half[0, i + 1]
        depth_east[i] = pltpu.roll(here, span - 1, 1)
        depth_west[i] = pltpu.roll(here, 1, 1)
        return carry

    lax.fori_loop(0, lead, shift_row, 0)

    def stencil(load, which, rate, transposed, i):
        acc = [None, None, None]
        rim = {}
        for c in range(3):
            x = load(c, pl.ds(i, BLOCK + 2))
            moved = (pltpu.roll(x, 1, 2), x, pltpu.roll(x, span - 1, 2))
            for dc in range(3):
                for dr in range(3):
                    view = moved[dc][dr:dr + BLOCK]
                    rim[c, dr, dc] = view
                    for o in range(3):
                        term = coefs[which, ((3 * dr + dc) * 3 + o) * 3 + c] * view
                        acc[o] = term if acc[o] is None else acc[o] + term
            drag = rate * friction[pl.ds(i, BLOCK)]
            if c:
                acc[c] = acc[c] - drag * rim[c, 1, 1]
            if transposed and c == 0:
                here = pl.ds(i, BLOCK)
                acc[1] = acc[1] + rate * (
                    depth_east[here] * rim[0, 1, 2] - depth_west[here] * rim[0, 1, 0]
                )
                acc[2] = acc[2] + rate * (
                    depth_half[0, pl.ds(i + 2, BLOCK)] * rim[0, 2, 1]
                    - depth_half[0, pl.ds(i, BLOCK)] * rim[0, 0, 1]
                )
        if not transposed:
            slope = (rim[1, 1, 2] - rim[1, 1, 0]) + (rim[2, 2, 1] - rim[2, 0, 1])
            acc[0] = acc[0] - rate * (depth_half[0, pl.ds(i + 1, BLOCK)] * slope)
        return [a * side[...] for a in acc]

    blocks = lead // BLOCK

    def adjoint_step(turn, carry):
        step = FINE - 1 - turn
        active = step < total

        def one(b, inner):
            i = b * BLOCK
            found = stencil(lambda c, at: adjoints[step + 1, c, at], 1, fine_rate, True, i)
            for c in range(3):
                old = adjoints[step + 1, c, pl.ds(i + 1, BLOCK)]
                adjoints[step, c, pl.ds(i + 1, BLOCK)] = jnp.where(active, found[c], old)
            return inner

        lax.fori_loop(0, blocks, one, 0)
        wrap(adjoints.at[step])
        return carry

    lax.fori_loop(0, FINE, adjoint_step, 0)

    def homeward(k):
        target = lax.rem(me + k, n)
        return pltpu.make_async_remote_copy(
            src_ref=back.at[:, :, pl.ds(pl.multiple_of(target * strip, strip), strip), :],
            dst_ref=landed.at[:, pl.ds(my_worker * own_tiles, own_tiles), :, :],
            send_sem=back_send.at[k],
            recv_sem=back_recv.at[k],
            device_id={"space": target},
            device_id_type=MESH,
        )

    def leads(device):
        return lax.rem(device, share) == 0

    def when(condition):
        return pl.when(condition) if share > 1 else (lambda f: f())

    def correct():
        for c in range(3):
            def change(i, carry):
                ending[c, i] = ending[c, i] - adjoints[FINE, c, i]
                return carry

            lax.fori_loop(0, lead + 2, change, 0)

        def one(b, carry):
            i = b * BLOCK
            found = stencil(lambda c, at: ending[c, at], 2, coarse_rate, True, i)
            for c in range(3):
                new_start[c, pl.ds(i + 1, BLOCK)] = (
                    found[c] + adjoints[0, c, pl.ds(i + 1, BLOCK)]
                )
            return carry

        lax.fori_loop(0, blocks, one, 0)
        wrap(new_start)

    def go_home():
        def row(i, carry):
            for c in range(3):
                for t in range(own_tiles):
                    back[c, t, pl.ds(i, 8, stride=lead), :] = new_start[
                        c, i + 1, :, t * LANES:(t + 1) * LANES
                    ]
            return carry

        lax.fori_loop(0, lead, row, 0)

        @when(leads(me))
        def _():
            for k in range(1, n):
                homeward(k).start()
            landed[:, pl.ds(my_worker * own_tiles, own_tiles)] = back[:, :, my_rows, :]

    def across():
        return pltpu.make_async_remote_copy(
            src_ref=new_start,
            dst_ref=ending,
            send_sem=cross_send,
            recv_sem=cross_recv,
            device_id={"cuts": lax.rem(cut + slices - 1, slices)},
            device_id_type=MESH,
        )

    @pl.when(last)
    def _():
        for c in range(3):
            def change(i, carry):
                ending[c, i] = adjoints[FINE, c, i]
                return carry

            lax.fori_loop(0, lead + 2, change, 0)
        correct()
        if slices > 1:
            across().start()
        go_home()

    for k in range(1, n):
        outward(send_state, recv_state, state_send, state_recv, k).wait_recv()
    spread(recv_state, states.at[0])

    def forward_step(step, carry):
        def one(b, inner):
            i = b * BLOCK
            found = stencil(lambda c, at: states[step, c, at], 0, fine_rate, False, i)
            for c in range(3):
                states[step + 1, c, pl.ds(i + 1, BLOCK)] = found[c]
            return inner

        lax.fori_loop(0, blocks, one, 0)
        wrap(states.at[step + 1])
        return carry

    lax.fori_loop(0, FINE - 1, forward_step, 0)

    if slices > 1:
        @pl.when(jnp.logical_not(last))
        def _():
            across().wait_recv()
            correct()
            go_home()

            @pl.when(cut > 0)
            def _():
                across().start()

    grad_scale = fine_rate * float(rows * cols * slices) ** (-0.5) / share
    zero = jnp.zeros((8, LANES), jnp.float32)
    own = own_tiles * LANES

    for c in range(3):
        def pairs(turn, sums):
            step = turn // (lead // GRAD_BLOCK)
            i = (turn % (lead // GRAD_BLOCK)) * GRAD_BLOCK
            factor = jnp.where(step < total, grad_scale, 0.0)
            x = states[step, c, pl.ds(i, GRAD_BLOCK + 2)]
            lam = [
                factor * adjoints[step + 1, o, pl.ds(i + 1, GRAD_BLOCK), :, 0:own]
                for o in range(3)
            ]
            moved = (pltpu.roll(x, 1, 2), x, pltpu.roll(x, span - 1, 2))
            result = []
            for dr in range(3):
                for dc in range(3):
                    view = moved[dc][dr:dr + GRAD_BLOCK, :, 0:own]
                    for o in range(3):
                        prod = view * lam[o]
                        part = sums[len(result)]
                        for r in range(GRAD_BLOCK):
                            for t in range(own_tiles):
                                part = part + prod[r, :, t * LANES:(t + 1) * LANES]
                        result.append(part)
            return tuple(result)

        sums = lax.fori_loop(0, FINE * (lead // GRAD_BLOCK), pairs, (zero,) * 27)
        for at in range(27):
            products[at * 3 + c] = sums[at]
    for at in range(81, products.shape[0]):
        products[at] = zero

    column = jnp.sum(jnp.sum(products[...], axis=1), axis=1, keepdims=True)
    count = products.shape[0]
    diagonal = lax.broadcasted_iota(jnp.int32, (count, LANES), 0) == lax.broadcasted_iota(
        jnp.int32, (count, LANES), 1
    )
    line = jnp.sum(jnp.where(diagonal, column, 0.0), axis=0, keepdims=True)
    grad_parts[0] = jnp.broadcast_to(line, (8, LANES))

    def share_grad(j):
        a, b = partners[j]
        return pltpu.make_async_remote_copy(
            src_ref=grad_parts.at[0],
            dst_ref=grad_parts.at[j + 1],
            send_sem=grad_send.at[j],
            recv_sem=grad_recv.at[j],
            device_id={"space": lax.rem(me + a, n), "cuts": lax.rem(cut + b, slices)},
            device_id_type=MESH,
        )

    for j in range(len(partners)):
        share_grad(j).start()

    for k in range(1, n):
        @when(leads(lax.rem(me + n - k, n)))
        def _():
            homeward(k).wait_recv()

    for t in range(cols // LANES):
        out_ref[0, :, :, t * LANES:(t + 1) * LANES] = landed[:, t]

    whole = grad_parts[0]
    for j in range(len(partners)):
        share_grad(j).wait_recv()
        whole = whole + grad_parts[j + 1]
    grad_ref[...] = whole

    for k in range(1, n):
        outward(send_adj, recv_adj, adj_send, adj_recv, k).wait_send()
        outward(send_state, recv_state, state_send, state_recv, k).wait_send()

    @when(leads(me))
    def _():
        for k in range(1, n):
            homeward(k).wait_send()

    if slices > 1:
        @pl.when(cut > 0)
        def _():
            across().wait_send()

    for j in range(len(partners)):
        share_grad(j).wait_send()


def body(depth_class, coef_table, step_counts, closure_weights, checkpoints, old_adjoint):
    n = lax.axis_size("space")
    slices = lax.axis_size("cuts")
    strip, cols = depth_class.shape
    rows = strip * n
    width = max(cols // n, LANES)
    share = width * n // cols
    tiles = width // LANES + 1
    span = tiles * LANES
    lead = rows // 8
    geo = (n, slices, strip, rows, cols, width, share)
    partners = n * slices - 1
    f32 = jnp.float32
    vmem = pl.BlockSpec(memory_space=pltpu.VMEM)
    smem = pl.BlockSpec(memory_space=pltpu.SMEM)
    dma = pltpu.SemaphoreType.DMA
    new_adjoint, grad = pl.pallas_call(
        functools.partial(kernel, geo),
        out_shape=(
            jax.ShapeDtypeStruct((1, 3, strip, cols), f32),
            jax.ShapeDtypeStruct((8, LANES), f32),
        ),
        in_specs=[vmem, smem, smem, smem, vmem, vmem],
        out_specs=(vmem, vmem),
        scratch_shapes=[
            pltpu.VMEM((n, 4 * tiles - 3, strip, LANES), f32),
            pltpu.VMEM((n, 3 * tiles - 2, strip, LANES), f32),
            pltpu.VMEM((4 * tiles - 3, rows, LANES), f32),
            pltpu.VMEM((3 * tiles - 2, rows, LANES), f32),
            pltpu.VMEM((1, lead + 2, 8, span), f32),
            pltpu.VMEM((lead, 8, span), f32),
            pltpu.VMEM((lead, 8, span), f32),
            pltpu.VMEM((lead, 8, span), f32),
            pltpu.VMEM((FINE, 3, lead + 2, 8, span), f32),
            pltpu.VMEM((FINE + 1, 3, lead + 2, 8, span), f32),
            pltpu.VMEM((3, lead + 2, 8, span), f32),
            pltpu.VMEM((3, lead + 2, 8, span), f32),
            pltpu.VMEM((3, tiles - 1, rows, LANES), f32),
            pltpu.VMEM((3, cols // LANES, strip, LANES), f32),
            pltpu.VMEM((88, 8, LANES), f32),
            pltpu.VMEM((partners + 1, 8, LANES), f32),
            pltpu.VMEM((8, span), f32),
            pltpu.SMEM((3, 81), f32),
            dma((n,)), dma((n,)), dma((n,)), dma((n,)),
            dma(()), dma(()),
            dma((n,)), dma((n,)),
            dma((partners,)), dma((partners,)),
        ],
        compiler_params=pltpu.CompilerParams(
            collective_id=0, has_side_effects=True, vmem_limit_bytes=48 * 1024 * 1024
        ),
    )(depth_class, coef_table, step_counts, closure_weights, checkpoints[0], old_adjoint[0])
    return new_adjoint, grad[0, :81].reshape(9, 3, 3)


def solution(mesh):
    return jax.shard_map(
        body,
        mesh=mesh,
        in_specs=(
            P("space", None),
            P(),
            P(),
            P("member", None, None),
            P(("member", "cuts"), None, "space", None),
            P(("member", "cuts"), None, "space", None),
        ),
        out_specs=(P(("member", "cuts"), None, "space", None), P("member", None, None)),
        check_vma=False,
    )
```
